32 devices in a mesh: grp: 4 (over z), seq: 8 (over y, x, core).
Axes of the slice: x: 2, y: 2, z: 4, core: 2. Of those that a mesh axis runs over, the one named last changes fastest.
Arguments:
- queries: bfloat16 [4, 4, 2, 128, 576], P('grp', None, None, 'seq'), may hold values from -1024 to 1024
- latent_cache: bfloat16 [4, 65536, 576], P(None, ('grp', 'seq')), may hold values from -6 to 6
- lengths: int32 [4], replicated, may hold values from 8192 to 65536
- owner_group: int32 [4], replicated, may hold values from 0 to 3, as said below
Outputs:
- attended: bfloat16 [4, 2, 128, 512], P(None, None, ('grp', 'seq'))
The draws below stay inside these ranges and needn't reach their ends.
Inputs may be any that keep to these rules, and one draw needn't show every extreme that they name: `owner_group`: each of 0 to 3 appears exactly once.
All inputs are finite; a program needn't handle non-finite values.
Results may differ from the reference program's by a relative error of at most 0.0015.
Values may be sent and summed in bfloat16 or wider, within the bound.
A program may use at most 64 MiB of HBM per device.

```python
import jax
import jax.numpy as jnp
from jax import lax

HEADS = 128
LATENT_WIDTH = 512
ROPE = 64
DRAFT = 2
BATCH = 4
CT = 2048
LEN = 65536
N_GRP = 4
N_SEQ = 8


score_factor = 192.0 ** (-0.5)


def special_rows(key):
    return jnp.clip(jax.random.normal(jax.random.fold_in(key, 11), (BATCH, 3, LATENT_WIDTH + ROPE), jnp.float32), -6.0, 6.0)


def nearby_rows(key):
    chosen = special_rows(key)
    direction = chosen / jnp.sum(chosen * chosen, axis=2, keepdims=True)
    amount = jax.random.uniform(jax.random.fold_in(key, 13), (BATCH, 3, 1), jnp.float32, 0.2, 1.0)
    return jnp.clip(chosen - 0.05 * amount * jnp.sum(chosen * chosen, axis=2, keepdims=True) * direction + 0.05 * jax.random.normal(jax.random.fold_in(key, 5), chosen.shape, jnp.float32), -6.0, 6.0)


def draw_latent_cache(key, part):
    drawn = jnp.clip(jax.random.normal(jax.random.fold_in(key, 3), (BATCH, LEN, LATENT_WIDTH + ROPE), jnp.float32), -6.0, 6.0)
    drawn = drawn.at[:, 0:6:2].set(special_rows(key))
    drawn = drawn.at[:, 1:6:2].set(nearby_rows(key))
    return drawn.astype(jnp.bfloat16)


def draw_queries(key, part):
    drawn = jnp.clip(jax.random.normal(jax.random.fold_in(key, 17), (N_GRP, BATCH, DRAFT, HEADS, LATENT_WIDTH + ROPE), jnp.float32), -6.0, 6.0)
    chosen = special_rows(key)
    norms = jnp.sum(chosen * chosen, axis=2, keepdims=True) * score_factor
    aligned = chosen / norms
    strengths = (120.0, 250.0, 400.0)
    for index in range(3):
        row = jnp.clip(strengths[index] * aligned[:, index, :], -1000.0, 1000.0)
        drawn = drawn.at[:, :, :, index].set(jnp.broadcast_to(row[None, :, None, :], (N_GRP, BATCH, DRAFT, LATENT_WIDTH + ROPE)))
    return drawn.astype(jnp.bfloat16)


def draw_owner_group(key, part):
    return jax.random.permutation(jax.random.fold_in(key, 29), N_GRP).astype(jnp.int32)


def with_ends(values, stream_key, least, high):
    shape = values.shape
    index_at = [jax.random.randint(jax.random.fold_in(stream_key, axis), (), 0, shape[axis]) for axis in range(len(shape))]
    values = values.at[tuple(index_at)].set(least)
    longest = shape.index(max(shape))
    index_at[longest] = (index_at[longest] + 1) % shape[longest]
    return values.at[tuple(index_at)].set(high)


def setup_inputs(seed: int = 0) -> dict:
    streams_of = jax.random.split(jax.random.key(seed), 5)
    queries = draw_queries(jax.random.fold_in(streams_of[4], 71), 0)
    latent_cache = draw_latent_cache(jax.random.fold_in(streams_of[4], 71), 0)
    lengths = with_ends(jax.random.randint(streams_of[2], (BATCH,), LEN // 8, LEN + 1), jax.random.fold_in(streams_of[2], 1), LEN // 8, LEN).astype(jnp.int32)
    owner_group = draw_owner_group(jax.random.fold_in(streams_of[4], 71), 0)
    return {"queries": queries, "latent_cache": latent_cache, "lengths": lengths, "owner_group": owner_group}


softmax_scale = 192.0 ** -0.5
masked_score = -1.0e30


def join(first, second):
    first_max, first_sum, first_out = first
    second_max, second_sum, second_out = second
    highest = jnp.maximum(first_max, second_max)
    first_scale = jnp.exp(first_max - highest)
    second_scale = jnp.exp(second_max - highest)
    return (highest, first_sum * first_scale + second_sum * second_scale,
            first_out * first_scale[..., None] + second_out * second_scale[..., None])


def block_partial(query_matrix, cache_block, limits, block_rank, blocks):
    batch, rows, width = query_matrix.shape
    slots = cache_block.shape[1]
    stripe = slots // 2
    drafts = limits.shape[1]
    heads = rows // drafts
    offset = jnp.arange(slots, dtype=jnp.int32)
    position = jnp.where(offset < stripe, block_rank * stripe + offset,
                         (2 * blocks - 1 - block_rank) * stripe + offset - stripe)
    valid_slot = position[None, None, :] < limits[:, :, None]
    logit_scores = jnp.einsum("fdi,fei->fde", query_matrix.astype(jnp.float32), cache_block.astype(jnp.float32)) * softmax_scale
    logit_scores = logit_scores.reshape(batch, drafts, heads, slots)
    logit_scores = jnp.where(valid_slot[:, :, None, :], logit_scores, masked_score)
    local_max = jnp.max(logit_scores, axis=3)
    weights = jnp.where(valid_slot[:, :, None, :], jnp.exp(logit_scores - local_max[..., None]), 0.0)
    local_sum = jnp.sum(weights, axis=3)
    rounded_values = weights.astype(jnp.bfloat16).reshape(batch, rows, slots)
    latent_rows = cache_block[:, :, :LATENT_WIDTH]
    partial_output = jnp.einsum("giv,gvu->giu", rounded_values.astype(jnp.float32), latent_rows.astype(jnp.float32))
    return local_max, local_sum, partial_output.reshape(batch, drafts, heads, LATENT_WIDTH)


def reference(queries, latent_cache, lengths, owner_group):
    row_index = jnp.arange(BATCH * DRAFT, dtype=jnp.int32) % N_GRP
    owners = jnp.take(owner_group.astype(jnp.int32), row_index).reshape(BATCH, DRAFT)
    picked = owners[None, :, :] == jnp.arange(N_GRP, dtype=jnp.int32)[:, None, None]
    chosen = jnp.sum(jnp.where(picked[:, :, :, None, None], queries.astype(jnp.float32), 0.0), axis=0).astype(jnp.bfloat16)
    query_matrix = chosen.reshape(BATCH, DRAFT * HEADS, LATENT_WIDTH + ROPE)
    limits = lengths[:, None].astype(jnp.int32) - DRAFT + 1 + jnp.arange(DRAFT, dtype=jnp.int32)[None, :]
    blocks = N_GRP * N_SEQ
    start = (jnp.full((BATCH, DRAFT, HEADS), masked_score, jnp.float32),
             jnp.zeros((BATCH, DRAFT, HEADS), jnp.float32),
             jnp.zeros((BATCH, DRAFT, HEADS, LATENT_WIDTH), jnp.float32))

    def visit(block_rank, carry):
        block_rank = jnp.asarray(block_rank).astype(jnp.int32)
        cache_block = lax.dynamic_slice_in_dim(latent_cache, block_rank * CT, CT, 1)
        return join(carry, block_partial(query_matrix, cache_block, limits, block_rank, blocks))

    highest, total, summed = lax.fori_loop(0, blocks, visit, start)
    return (summed / total[..., None]).astype(jnp.bfloat16)
```

```python
import functools

import jax
import jax.numpy as jnp
import numpy as np
from jax import lax
from jax.experimental import pallas as pl
from jax.experimental.pallas import tpu as pltpu
from jax.sharding import PartitionSpec as P

LATENT_WIDTH = 512
LOG2E = 1.4426950408889634
MESH = pl.DeviceIdType.MESH
TAIL = 128


softmax_scale = 192.0 ** (-0.5)
masked_score = -1e30


def merge(parts, latent):
    tops = [part[..., latent + TAIL // 2 : latent + TAIL // 2 + 1] for part in parts]
    top = functools.reduce(jnp.maximum, tops)
    total, output = None, None
    for part, own_top in zip(parts, tops):
        factor = jnp.exp2(own_top - top)
        part_sum = part[..., latent : latent + 1] * factor
        part_output = part[..., :latent] * factor
        total = part_sum if total is None else total + part_sum
        output = part_output if output is None else output + part_output
    return top, total, output


def pack_tail(top, total):
    shape = top.shape[:-1] + (TAIL,)
    lane = lax.broadcasted_iota(jnp.int32, shape, len(shape) - 1)
    return jnp.where(
        lane < TAIL // 2, jnp.broadcast_to(total, shape), jnp.broadcast_to(top, shape)
    )


def fused_kernel(dims, lengths_ref, owner_ref, query_ref, order_ref, cache_ref, out_ref, *scratch):
    batch, drafts, groups, seqs, chunks, heads_per, slots, width, latent = dims
    chips = seqs // 2
    per_chunk = batch // chunks
    rows_per = drafts * heads_per
    rows = drafts * heads_per * groups * seqs
    gathered = scratch[:chunks]
    (cache, query, packed, core_in, plane_out, plane_in, group_out, group_in) = scratch[
        chunks : chunks + 8
    ]
    (
        cache_sem,
        zq_send, zq_recv, pq_send, pq_recv, sq_send, sq_recv,
        c_send, c_recv, p_send, p_recv, z_send, z_recv,
    ) = scratch[chunks + 8 :]

    grp = lax.axis_index("grp")
    seq = lax.axis_index("seq")
    core = lax.rem(seq, 2)
    chip = seq // 2
    sibling = seq + 1 - 2 * core

    def group_peer(step):
        return lax.rem(grp + step, groups)

    def chip_peer(step):
        return lax.rem(chip + step, chips)

    def cache_copy(b):
        return pltpu.make_async_copy(cache_ref.at[b], cache.at[b], cache_sem.at[b])

    for b in range(batch):
        cache_copy(b).start()

    peers = [(group_peer(k), seq) for k in range(1, groups)]
    peers += [(grp, chip_peer(k) * 2 + core) for k in range(1, chips)]
    peers += [(grp, sibling)]
    barrier = pltpu.get_barrier_semaphore()
    for peer in peers:
        pl.semaphore_signal(barrier, inc=1, device_id=peer, device_id_type=MESH)

    held = jnp.int32(0)
    for k in range(groups):
        held = jnp.where(owner_ref[k] == grp, k, held)
    for n in range(chunks):
        gathered[n][seq, grp] = query_ref[n, held]
    pl.semaphore_wait(barrier, len(peers))

    def remote(src, dst, send, recv, peer):
        return pltpu.make_async_remote_copy(
            src_ref=src, dst_ref=dst, send_sem=send, recv_sem=recv,
            device_id=peer, device_id_type=MESH,
        )

    def zq(n, k):
        ref = gathered[n].at[seq, grp]
        return remote(ref, ref, zq_send.at[n, k - 1], zq_recv.at[n, k - 1], (group_peer(k), seq))

    def pq(n, k):
        ref = gathered[n].at[seq]
        return remote(
            ref, ref, pq_send.at[n, k - 1], pq_recv.at[n, k - 1], (grp, chip_peer(k) * 2 + core)
        )

    def sq(n, k):
        ref = gathered[n].at[chip_peer(chips - k) * 2 + core]
        return remote(ref, ref, sq_send.at[n, k], sq_recv.at[n, k], (grp, sibling))

    def c_copy(b):
        return remote(
            packed.at[b, 1 - core], core_in.at[b], c_send.at[b], c_recv.at[b], (grp, sibling)
        )

    def p_copy(b, k):
        return remote(
            plane_out.at[b, chip_peer(k)], plane_in.at[b, k - 1],
            p_send.at[b, k - 1], p_recv.at[b, k - 1], (grp, chip_peer(k) * 2 + core),
        )

    def z_copy(b, k):
        return remote(
            group_out.at[b, group_peer(k)], group_in.at[b, k - 1],
            z_send.at[b, k - 1], z_recv.at[b, k - 1], (group_peer(k), seq),
        )

    def forward(n):
        for k in range(1, chips):
            pq(n, k).wait_recv()
            sq(n, k).start()

    for n in range(chunks):
        for k in range(1, groups):
            zq(n, k).start()
    for n in range(chunks):
        for k in range(1, groups):
            zq(n, k).wait_recv()
        for k in range(1, chips):
            pq(n, k).start()
        sq(n, 0).start()
    forward(0)

    blocks = groups * seqs
    rank = grp * seqs + seq
    stripe = slots // 2
    log_scale = softmax_scale * LOG2E

    def step(b, carry):
        @pl.when(b < batch)
        def _():
            for n in range(chunks):
                @pl.when(b == n * per_chunk)
                def _():
                    for k in range(chips):
                        sq(n, k).wait_recv()

                @pl.when(b // per_chunk == n)
                def _():
                    whole = []
                    for t in range(drafts):
                        row = b * drafts + t
                        owner = owner_ref[lax.rem(row, groups)]
                        whole.append(gathered[n][:, owner].reshape(rows // drafts, width))
                    stacked = jnp.concatenate(whole, axis=0)
                    query[...] = jnp.dot(
                        order_ref[...], stacked, preferred_element_type=jnp.float32
                    ).astype(jnp.bfloat16)

            cache_copy(b).wait()
            scores = lax.dot_general(
                query[...], cache[b], (((1,), (1,)), ((), ())),
                preferred_element_type=jnp.float32,
            )
            offset = lax.broadcasted_iota(jnp.int32, (1, slots), 1)
            position = jnp.where(
                offset < stripe,
                rank * stripe + offset,
                (2 * blocks - 1 - rank) * stripe + offset - stripe,
            )
            row_index = lax.broadcasted_iota(jnp.int32, (rows, 1), 0)
            draft = lax.rem(row_index, rows_per) // heads_per
            limit = lengths_ref[b] - drafts + 1 + draft
            scores = jnp.where(position < limit, scores, masked_score)
            top = jnp.maximum(jnp.max(scores, axis=1, keepdims=True), 0.1 * masked_score)
            weights = jnp.exp2((scores - top) * log_scale)
            total = jnp.sum(weights, axis=1, keepdims=True)
            output = jnp.dot(
                weights.astype(jnp.bfloat16), cache[b, :, :latent],
                preferred_element_type=jnp.float32,
            )
            split = (2, chips, groups * rows_per)
            packed[b, :, :, :, :latent] = output.reshape(split + (latent,))
            packed[b, :, :, :, latent:] = pack_tail(top * log_scale, total).reshape(split + (TAIL,))
            c_copy(b).start()

            for n in range(1, chunks):
                @pl.when(b == n * per_chunk - 1)
                def _():
                    forward(n)

        @pl.when((b >= 1) & (b < batch + 1))
        def _():
            at = b - 1
            c_copy(at).wait_recv()
            top, total, output = merge([packed[at, core], core_in[at]], latent)
            plane_out[at, :, :, :latent] = output
            plane_out[at, :, :, latent:] = pack_tail(top, total)
            for k in range(1, chips):
                p_copy(at, k).start()

        @pl.when((b >= 2) & (b < batch + 2))
        def _():
            at = b - 2
            for k in range(1, chips):
                p_copy(at, k).wait_recv()
            parts = [plane_out[at, chip]] + [plane_in[at, k] for k in range(chips - 1)]
            top, total, output = merge(parts, latent)
            group_out[at, :, :, :latent] = output.reshape(groups, rows_per, latent)
            group_out[at, :, :, latent:] = pack_tail(top, total).reshape(groups, rows_per, TAIL)
            for k in range(1, groups):
                z_copy(at, k).start()

        @pl.when(b >= 3)
        def _():
            at = b - 3
            for k in range(1, groups):
                z_copy(at, k).wait_recv()
            parts = [group_out[at, grp]] + [group_in[at, k] for k in range(groups - 1)]
            top, total, output = merge(parts, latent)
            out_ref[at] = output / total
            c_copy(at).wait_send()
            for k in range(1, chips):
                p_copy(at, k).wait_send()
            for k in range(1, groups):
                z_copy(at, k).wait_send()

        return carry

    lax.fori_loop(0, batch + 3, step, 0)
    for n in range(chunks):
        for k in range(1, groups):
            zq(n, k).wait_send()
        for k in range(1, chips):
            pq(n, k).wait_send()
        for k in range(chips):
            sq(n, k).wait_send()


def row_order(drafts, groups, seqs, heads_per):
    heads = groups * seqs * heads_per
    source = np.arange(drafts * heads).reshape(drafts, groups, seqs // 2, 2, heads_per)
    source = source.transpose(3, 2, 1, 0, 4).reshape(-1)
    return (source[:, None] == np.arange(drafts * heads)[None, :]).astype(np.float32)


def fused_shards(queries, latent_cache, lengths, owner_group):
    seqs = lax.axis_size("seq")
    groups = lax.axis_size("grp")
    _, batch, drafts, part_heads, width = queries.shape
    slots = latent_cache.shape[1]
    latent = LATENT_WIDTH
    heads_per = part_heads // groups
    chunks = batch * drafts // groups
    chips = seqs // 2
    rows_per = drafts * heads_per
    rows = rows_per * groups * seqs
    dims = (batch, drafts, groups, seqs, chunks, heads_per, slots, width, latent)
    wide = latent + TAIL
    order = jnp.asarray(row_order(drafts, groups, seqs, heads_per), jnp.bfloat16)
    f32, bf16 = jnp.float32, jnp.bfloat16
    dma = pltpu.SemaphoreType.DMA
    out = pl.pallas_call(
        functools.partial(fused_kernel, dims),
        out_shape=jax.ShapeDtypeStruct((batch, rows_per, latent), f32),
        in_specs=[
            pl.BlockSpec(memory_space=pltpu.SMEM),
            pl.BlockSpec(memory_space=pltpu.SMEM),
            pl.BlockSpec(memory_space=pltpu.VMEM),
            pl.BlockSpec(memory_space=pltpu.VMEM),
            pl.BlockSpec(memory_space=pl.ANY),
        ],
        out_specs=pl.BlockSpec(memory_space=pltpu.VMEM),
        scratch_shapes=[pltpu.VMEM((seqs, groups, part_heads, width), bf16)] * chunks
        + [
            pltpu.VMEM((batch, slots, width), bf16),
            pltpu.VMEM((rows, width), bf16),
            pltpu.VMEM((batch, 2, chips, groups * rows_per, wide), f32),
            pltpu.VMEM((batch, chips, groups * rows_per, wide), f32),
            pltpu.VMEM((batch, chips, groups * rows_per, wide), f32),
            pltpu.VMEM((batch, chips - 1, groups * rows_per, wide), f32),
            pltpu.VMEM((batch, groups, rows_per, wide), f32),
            pltpu.VMEM((batch, groups - 1, rows_per, wide), f32),
            dma((batch,)),
            dma((chunks, groups - 1)), dma((chunks, groups - 1)),
            dma((chunks, chips - 1)), dma((chunks, chips - 1)),
            dma((chunks, chips)), dma((chunks, chips)),
            dma((batch,)), dma((batch,)),
            dma((batch, chips - 1)), dma((batch, chips - 1)),
            dma((batch, groups - 1)), dma((batch, groups - 1)),
        ],
        compiler_params=pltpu.CompilerParams(
            collective_id=0, has_side_effects=True, vmem_limit_bytes=48 * 1024 * 1024
        ),
    )(lengths, owner_group, queries.reshape(chunks, groups, part_heads, width), order, latent_cache)
    return out.reshape(batch, drafts, heads_per, latent).astype(bf16)


def fits_kernel(mesh):
    seqs, groups = mesh.shape["seq"], mesh.shape["grp"]

    def check(queries):
        _, batch, drafts, heads, _ = queries.shape
        parts = seqs * groups
        rows = batch * drafts
        return (
            seqs % 2 == 0 and seqs > 2 and groups > 1
            and heads % parts == 0 and (heads // parts * drafts) % 8 == 0
            and (heads // seqs) % 16 == 0
            and rows % groups == 0 and batch % (rows // groups) == 0
        )

    return check


def block_partial(query_matrix, cache_block, limits, block_rank, blocks):
    batch, rows, width = query_matrix.shape
    slots = cache_block.shape[1]
    stripe = slots // 2
    drafts = limits.shape[1]
    heads = rows // drafts
    offset = jnp.arange(slots, dtype=jnp.int32)
    position = jnp.where(
        offset < stripe,
        block_rank * stripe + offset,
        (2 * blocks - 1 - block_rank) * stripe + offset - stripe,
    )
    valid_slot = position[None, None, :] < limits[:, :, None]
    logit_scores = (
        jnp.einsum("fdi,fei->fde", query_matrix, cache_block, preferred_element_type=jnp.float32)
        * softmax_scale
    )
    logit_scores = logit_scores.reshape(batch, drafts, heads, slots)
    logit_scores = jnp.where(valid_slot[:, :, None, :], logit_scores, masked_score)
    local_max = jnp.max(logit_scores, axis=3)
    weights = jnp.where(
        valid_slot[:, :, None, :], jnp.exp(logit_scores - local_max[..., None]), 0.0
    )
    local_sum = jnp.sum(weights, axis=3)
    rounded_values = weights.astype(jnp.bfloat16).reshape(batch, rows, slots)
    partial_output = jnp.einsum(
        "giv,gvu->giu",
        rounded_values,
        cache_block[:, :, :LATENT_WIDTH],
        preferred_element_type=jnp.float32,
    )
    return (local_max, local_sum, partial_output.reshape(batch, drafts, heads, LATENT_WIDTH))


def owned_rows(copies, owner_group, group_count, group_rank):
    batch, drafts = (copies.shape[1], copies.shape[2])
    row_index = jnp.arange(batch * drafts, dtype=jnp.int32) % group_count
    owners = jnp.take(owner_group, row_index).reshape(batch, drafts)
    mine = owners == group_rank
    return jnp.where(mine[None, :, :, None, None], copies.astype(jnp.float32), 0.0)


def shards(queries, latent_cache, lengths, owner_group):
    seq_count = lax.axis_size("seq")
    group_count = lax.axis_size("grp")
    blocks = seq_count * group_count
    group_rank = lax.axis_index("grp")
    device_rank = group_rank * seq_count + lax.axis_index("seq")
    kept = owned_rows(queries, owner_group, group_count, group_rank)
    own_heads = lax.psum(kept.astype(jnp.bfloat16), "grp")
    gathered = lax.all_gather(own_heads, "seq", axis=3, tiled=True)
    batch, drafts, heads, width = gathered.shape[1:]
    query_matrix = gathered.reshape(batch, drafts * heads, width)
    limits = lengths[:, None] - drafts + 1 + jnp.arange(drafts, dtype=jnp.int32)[None, :]
    local_parts = block_partial(query_matrix, latent_cache, limits, device_rank, blocks)
    local_max, local_sum, partial_output = local_parts
    highest = lax.pmax(local_max, ("grp", "seq"))
    factor = jnp.exp(local_max - highest)
    total, summed = (
        lax.psum_scatter(local_sum * factor, ("grp", "seq"), scatter_dimension=2, tiled=True),
        lax.psum_scatter(
            partial_output * factor[..., None], ("grp", "seq"), scatter_dimension=2, tiled=True
        ),
    )
    return (summed / total[..., None]).astype(jnp.bfloat16)


def solution(mesh):
    check = fits_kernel(mesh)

    def attend(queries, latent_cache, lengths, owner_group):
        return jax.shard_map(
            fused_shards if check(queries) else shards,
            mesh=mesh,
            in_specs=(P("grp", None, None, "seq", None), P(None, ("grp", "seq"), None), P(), P()),
            out_specs=P(None, None, ("grp", "seq"), None),
            check_vma=False,
        )(queries, latent_cache, lengths, owner_group)

    return attend
```

```python
import functools

import jax
import jax.numpy as jnp
import numpy as np
from jax import lax
from jax.experimental import pallas as pl
from jax.experimental.pallas import tpu as pltpu
from jax.sharding import PartitionSpec as P

LATENT_WIDTH = 512
LOG2E = 1.4426950408889634
MESH = pl.DeviceIdType.MESH
TAIL = 128


softmax_scale = 192.0 ** (-0.5)
masked_score = -1e30


def merge(parts, latent):
    tops = [part[..., latent + TAIL // 2 : latent + TAIL // 2 + 1] for part in parts]
    top = functools.reduce(jnp.maximum, tops)
    total, output = None, None
    for part, own_top in zip(parts, tops):
        factor = jnp.exp2(own_top - top)
        part_sum = part[..., latent : latent + 1] * factor
        part_output = part[..., :latent] * factor
        total = part_sum if total is None else total + part_sum
        output = part_output if output is None else output + part_output
    return top, total, output


def pack_tail(top, total):
    shape = top.shape[:-1] + (TAIL,)
    lane = lax.broadcasted_iota(jnp.int32, shape, len(shape) - 1)
    return jnp.where(
        lane < TAIL // 2, jnp.broadcast_to(total, shape), jnp.broadcast_to(top, shape)
    )


def fused_kernel(dims, lengths_ref, owner_ref, query_ref, order_ref, cache_ref, out_ref, *scratch):
    batch, drafts, groups, seqs, chunks, heads_per, slots, width, latent = dims
    chips = seqs // 2
    per_chunk = batch // chunks
    rows_per = drafts * heads_per
    rows = drafts * heads_per * groups * seqs
    gathered = scratch[:chunks]
    (cache, query, packed, core_in, plane_out, plane_in, group_out, group_in) = scratch[
        chunks : chunks + 8
    ]
    (
        cache_sem,
        zq_send, zq_recv, pq_send, pq_recv, sq_send, sq_recv,
        c_send, c_recv, p_send, p_recv, z_send, z_recv,
    ) = scratch[chunks + 8 :]

    grp = lax.axis_index("grp")
    seq = lax.axis_index("seq")
    core = lax.rem(seq, 2)
    chip = seq // 2
    sibling = seq + 1 - 2 * core

    def group_peer(step):
        return lax.rem(grp + step, groups)

    def chip_peer(step):
        return lax.rem(chip + step, chips)

    def cache_copy(b):
        return pltpu.make_async_copy(cache_ref.at[b], cache.at[b], cache_sem.at[b])

    for b in range(batch):
        cache_copy(b).start()

    peers = [(group_peer(k), seq) for k in range(1, groups)]
    peers += [(grp, chip_peer(k) * 2 + core) for k in range(1, chips)]
    peers += [(grp, sibling)]
    barrier = pltpu.get_barrier_semaphore()
    for peer in peers:
        pl.semaphore_signal(barrier, inc=1, device_id=peer, device_id_type=MESH)

    held = jnp.int32(0)
    for k in range(groups):
        held = jnp.where(owner_ref[k] == grp, k, held)
    for n in range(chunks):
        gathered[n][seq, grp] = query_ref[n, held]
    pl.semaphore_wait(barrier, len(peers))

    def remote(src, dst, send, recv, peer):
        return pltpu.make_async_remote_copy(
            src_ref=src, dst_ref=dst, send_sem=send, recv_sem=recv,
            device_id=peer, device_id_type=MESH,
        )

    def zq(n, k):
        ref = gathered[n].at[seq, grp]
        return remote(ref, ref, zq_send.at[n, k - 1], zq_recv.at[n, k - 1], (group_peer(k), seq))

    def pq(n, k):
        ref = gathered[n].at[seq]
        return remote(
            ref, ref, pq_send.at[n, k - 1], pq_recv.at[n, k - 1], (grp, chip_peer(k) * 2 + core)
        )

    def sq(n, k):
        ref = gathered[n].at[chip_peer(chips - k) * 2 + core]
        return remote(ref, ref, sq_send.at[n, k], sq_recv.at[n, k], (grp, sibling))

    def c_copy(b):
        return remote(
            packed.at[b, 1 - core], core_in.at[b], c_send.at[b], c_recv.at[b], (grp, sibling)
        )

    def p_copy(b, k):
        return remote(
            plane_out.at[b, chip_peer(k)], plane_in.at[b, k - 1],
            p_send.at[b, k - 1], p_recv.at[b, k - 1], (grp, chip_peer(k) * 2 + core),
        )

    def z_copy(b, k):
        return remote(
            group_out.at[b, group_peer(k)], group_in.at[b, k - 1],
            z_send.at[b, k - 1], z_recv.at[b, k - 1], (group_peer(k), seq),
        )

    def forward(n):
        for k in range(1, chips):
            pq(n, k).wait_recv()
            sq(n, k).start()

    for k in range(1, groups):
        zq(0, k).start()
    for n in range(chunks):
        for k in range(1, groups):
            zq(n, k).wait_recv()
        for k in range(1, chips):
            pq(n, k).start()
        sq(n, 0).start()
        if n + 1 < chunks:
            for k in range(1, groups):
                zq(n + 1, k).start()
        if n == 0:
            forward(0)

    blocks = groups * seqs
    rank = grp * seqs + seq
    stripe = slots // 2
    log_scale = softmax_scale * LOG2E

    def plane_stage(at):
        c_copy(at).wait_recv()
        top, total, output = merge([packed[at, core], core_in[at]], latent)
        plane_out[at, :, :, :latent] = output
        plane_out[at, :, :, latent:] = pack_tail(top, total)
        for k in range(1, chips):
            p_copy(at, k).start()

    def step(b, carry):
        @pl.when(b < batch)
        def _():
            for n in range(chunks):
                @pl.when(b == n * per_chunk)
                def _():
                    for k in range(chips):
                        sq(n, k).wait_recv()

                @pl.when(b // per_chunk == n)
                def _():
                    whole = []
                    for t in range(drafts):
                        row = b * drafts + t
                        owner = owner_ref[lax.rem(row, groups)]
                        whole.append(gathered[n][:, owner].reshape(rows // drafts, width))
                    stacked = jnp.concatenate(whole, axis=0)
                    query[...] = jnp.dot(
                        order_ref[...], stacked, preferred_element_type=jnp.float32
                    ).astype(jnp.bfloat16)

            cache_copy(b).wait()
            scores = jnp.dot(query[...], cache[b], preferred_element_type=jnp.float32)

            @pl.when(b >= 1)
            def _():
                plane_stage(b - 1)

            offset = lax.broadcasted_iota(jnp.int32, (1, slots), 1)
            position = jnp.where(
                offset < stripe,
                rank * stripe + offset,
                (2 * blocks - 1 - rank) * stripe + offset - stripe,
            )
            row_index = lax.broadcasted_iota(jnp.int32, (rows, 1), 0)
            draft = lax.rem(row_index, rows_per) // heads_per
            limit = lengths_ref[b] - drafts + 1 + draft
            scores = jnp.where(position < limit, scores, masked_score)
            top = jnp.maximum(jnp.max(scores, axis=1, keepdims=True), 0.1 * masked_score)
            weights = jnp.exp2((scores - top) * log_scale)
            total = jnp.sum(weights, axis=1, keepdims=True)
            output = lax.dot_general(
                weights.astype(jnp.bfloat16), cache[b, :latent], (((1,), (1,)), ((), ())),
                preferred_element_type=jnp.float32,
            )
            split = (2, chips, groups * rows_per)
            packed[b, :, :, :, :latent] = output.reshape(split + (latent,))
            packed[b, :, :, :, latent:] = pack_tail(top * log_scale, total).reshape(split + (TAIL,))
            c_copy(b).start()

            for n in range(1, chunks):
                @pl.when(b == n * per_chunk - 1)
                def _():
                    forward(n)

        @pl.when(b == batch)
        def _():
            plane_stage(b - 1)

        @pl.when((b >= 2) & (b < batch + 2))
        def _():
            at = b - 2
            for k in range(1, chips):
                p_copy(at, k).wait_recv()
            parts = [plane_out[at, chip]] + [plane_in[at, k] for k in range(chips - 1)]
            top, total, output = merge(parts, latent)
            group_out[at, :, :, :latent] = output.reshape(groups, rows_per, latent)
            group_out[at, :, :, latent:] = pack_tail(top, total).reshape(groups, rows_per, TAIL)
            for k in range(1, groups):
                z_copy(at, k).start()

        @pl.when(b >= 3)
        def _():
            at = b - 3
            for k in range(1, groups):
                z_copy(at, k).wait_recv()
            parts = [group_out[at, grp]] + [group_in[at, k] for k in range(groups - 1)]
            top, total, output = merge(parts, latent)
            out_ref[at] = output / total
            c_copy(at).wait_send()
            for k in range(1, chips):
                p_copy(at, k).wait_send()
            for k in range(1, groups):
                z_copy(at, k).wait_send()

        return carry

    lax.fori_loop(0, batch + 3, step, 0)
    for n in range(chunks):
        for k in range(1, groups):
            zq(n, k).wait_send()
        for k in range(1, chips):
            pq(n, k).wait_send()
        for k in range(chips):
            sq(n, k).wait_send()


def row_order(drafts, groups, seqs, heads_per):
    heads = groups * seqs * heads_per
    source = np.arange(drafts * heads).reshape(drafts, groups, seqs // 2, 2, heads_per)
    source = source.transpose(3, 2, 1, 0, 4).reshape(-1)
    return (source[:, None] == np.arange(drafts * heads)[None, :]).astype(np.float32)


def fused_shards(queries, latent_cache, lengths, owner_group):
    seqs = lax.axis_size("seq")
    groups = lax.axis_size("grp")
    _, batch, drafts, part_heads, width = queries.shape
    slots = latent_cache.shape[1]
    latent = LATENT_WIDTH
    heads_per = part_heads // groups
    chunks = batch * drafts // groups
    chips = seqs // 2
    rows_per = drafts * heads_per
    rows = rows_per * groups * seqs
    dims = (batch, drafts, groups, seqs, chunks, heads_per, slots, width, latent)
    wide = latent + TAIL
    order = jnp.asarray(row_order(drafts, groups, seqs, heads_per), jnp.bfloat16)
    f32, bf16 = jnp.float32, jnp.bfloat16
    dma = pltpu.SemaphoreType.DMA
    out = pl.pallas_call(
        functools.partial(fused_kernel, dims),
        out_shape=jax.ShapeDtypeStruct((batch, rows_per, latent), f32),
        in_specs=[
            pl.BlockSpec(memory_space=pltpu.SMEM),
            pl.BlockSpec(memory_space=pltpu.SMEM),
            pl.BlockSpec(memory_space=pltpu.VMEM),
            pl.BlockSpec(memory_space=pltpu.VMEM),
            pl.BlockSpec(memory_space=pl.ANY),
        ],
        out_specs=pl.BlockSpec(memory_space=pltpu.VMEM),
        scratch_shapes=[pltpu.VMEM((seqs, groups, part_heads, width), bf16)] * chunks
        + [
            pltpu.VMEM((batch, width, slots), bf16),
            pltpu.VMEM((rows, width), bf16),
            pltpu.VMEM((batch, 2, chips, groups * rows_per, wide), f32),
            pltpu.VMEM((batch, chips, groups * rows_per, wide), f32),
            pltpu.VMEM((batch, chips, groups * rows_per, wide), f32),
            pltpu.VMEM((batch, chips - 1, groups * rows_per, wide), f32),
            pltpu.VMEM((batch, groups, rows_per, wide), f32),
            pltpu.VMEM((batch, groups - 1, rows_per, wide), f32),
            dma((batch,)),
            dma((chunks, groups - 1)), dma((chunks, groups - 1)),
            dma((chunks, chips - 1)), dma((chunks, chips - 1)),
            dma((chunks, chips)), dma((chunks, chips)),
            dma((batch,)), dma((batch,)),
            dma((batch, chips - 1)), dma((batch, chips - 1)),
            dma((batch, groups - 1)), dma((batch, groups - 1)),
        ],
        compiler_params=pltpu.CompilerParams(
            collective_id=0, has_side_effects=True, vmem_limit_bytes=48 * 1024 * 1024
        ),
    )(lengths, owner_group, queries.reshape(chunks, groups, part_heads, width), order, latent_cache.transpose(0, 2, 1))
    return out.reshape(batch, drafts, heads_per, latent).astype(bf16)


def fits_kernel(mesh):
    seqs, groups = mesh.shape["seq"], mesh.shape["grp"]

    def check(queries):
        _, batch, drafts, heads, _ = queries.shape
        parts = seqs * groups
        rows = batch * drafts
        return (
            seqs % 2 == 0 and seqs > 2 and groups > 1
            and heads % parts == 0 and (heads // parts * drafts) % 8 == 0
            and (heads // seqs) % 16 == 0
            and rows % groups == 0 and batch % (rows // groups) == 0
        )

    return check


def block_partial(query_matrix, cache_block, limits, block_rank, blocks):
    batch, rows, width = query_matrix.shape
    slots = cache_block.shape[1]
    stripe = slots // 2
    drafts = limits.shape[1]
    heads = rows // drafts
    offset = jnp.arange(slots, dtype=jnp.int32)
    position = jnp.where(
        offset < stripe,
        block_rank * stripe + offset,
        (2 * blocks - 1 - block_rank) * stripe + offset - stripe,
    )
    valid_slot = position[None, None, :] < limits[:, :, None]
    logit_scores = (
        jnp.einsum("fdi,fei->fde", query_matrix, cache_block, preferred_element_type=jnp.float32)
        * softmax_scale
    )
    logit_scores = logit_scores.reshape(batch, drafts, heads, slots)
    logit_scores = jnp.where(valid_slot[:, :, None, :], logit_scores, masked_score)
    local_max = jnp.max(logit_scores, axis=3)
    weights = jnp.where(
        valid_slot[:, :, None, :], jnp.exp(logit_scores - local_max[..., None]), 0.0
    )
    local_sum = jnp.sum(weights, axis=3)
    rounded_values = weights.astype(jnp.bfloat16).reshape(batch, rows, slots)
    partial_output = jnp.einsum(
        "giv,gvu->giu",
        rounded_values,
        cache_block[:, :, :LATENT_WIDTH],
        preferred_element_type=jnp.float32,
    )
    return (local_max, local_sum, partial_output.reshape(batch, drafts, heads, LATENT_WIDTH))


def owned_rows(copies, owner_group, group_count, group_rank):
    batch, drafts = (copies.shape[1], copies.shape[2])
    row_index = jnp.arange(batch * drafts, dtype=jnp.int32) % group_count
    owners = jnp.take(owner_group, row_index).reshape(batch, drafts)
    mine = owners == group_rank
    return jnp.where(mine[None, :, :, None, None], copies.astype(jnp.float32), 0.0)


def shards(queries, latent_cache, lengths, owner_group):
    seq_count = lax.axis_size("seq")
    group_count = lax.axis_size("grp")
    blocks = seq_count * group_count
    group_rank = lax.axis_index("grp")
    device_rank = group_rank * seq_count + lax.axis_index("seq")
    kept = owned_rows(queries, owner_group, group_count, group_rank)
    own_heads = lax.psum(kept.astype(jnp.bfloat16), "grp")
    gathered = lax.all_gather(own_heads, "seq", axis=3, tiled=True)
    batch, drafts, heads, width = gathered.shape[1:]
    query_matrix = gathered.reshape(batch, drafts * heads, width)
    limits = lengths[:, None] - drafts + 1 + jnp.arange(drafts, dtype=jnp.int32)[None, :]
    local_parts = block_partial(query_matrix, latent_cache, limits, device_rank, blocks)
    local_max, local_sum, partial_output = local_parts
    highest = lax.pmax(local_max, ("grp", "seq"))
    factor = jnp.exp(local_max - highest)
    total, summed = (
        lax.psum_scatter(local_sum * factor, ("grp", "seq"), scatter_dimension=2, tiled=True),
        lax.psum_scatter(
            partial_output * factor[..., None], ("grp", "seq"), scatter_dimension=2, tiled=True
        ),
    )
    return (summed / total[..., None]).astype(jnp.bfloat16)


def solution(mesh):
    check = fits_kernel(mesh)

    def attend(queries, latent_cache, lengths, owner_group):
        return jax.shard_map(
            fused_shards if check(queries) else shards,
            mesh=mesh,
            in_specs=(P("grp", None, None, "seq", None), P(None, ("grp", "seq"), None), P(), P()),
            out_specs=P(None, None, ("grp", "seq"), None),
            check_vma=False,
        )(queries, latent_cache, lengths, owner_group)

    return attend
```

```python
import functools

import jax
import jax.numpy as jnp
import numpy as np
from jax import lax
from jax.experimental import pallas as pl
from jax.experimental.pallas import tpu as pltpu
from jax.sharding import PartitionSpec as P

LATENT_WIDTH = 512
LOG2E = 1.4426950408889634
MESH = pl.DeviceIdType.MESH
TAIL = 128


softmax_scale = 192.0 ** (-0.5)
masked_score = -1e30


def merge(parts, latent):
    tops = [part[..., latent + TAIL // 2 : latent + TAIL // 2 + 1] for part in parts]
    top = functools.reduce(jnp.maximum, tops)
    total, output = None, None
    for part, own_top in zip(parts, tops):
        factor = jnp.exp2(own_top - top)
        part_sum = part[..., latent : latent + 1] * factor
        part_output = part[..., :latent] * factor
        total = part_sum if total is None else total + part_sum
        output = part_output if output is None else output + part_output
    return top, total, output


def pack_tail(top, total):
    shape = top.shape[:-1] + (TAIL,)
    lane = lax.broadcasted_iota(jnp.int32, shape, len(shape) - 1)
    return jnp.where(
        lane < TAIL // 2, jnp.broadcast_to(total, shape), jnp.broadcast_to(top, shape)
    )


def fused_kernel(dims, lengths_ref, owner_ref, query_ref, order_ref, cache_ref, out_ref, *scratch):
    batch, drafts, groups, seqs, chunks, heads_per, slots, width, latent = dims
    chips = seqs // 2
    per_chunk = batch // chunks
    rows_per = drafts * heads_per
    rows = drafts * heads_per * groups * seqs
    gathered = scratch[:chunks]
    (
        cache, query, packed, core_in, plane_out, tail_in, code_out, code_in, group_out, group_in,
    ) = scratch[chunks : chunks + 10]
    (
        cache_sem,
        zq_send, zq_recv, pq_send, pq_recv, sq_send, sq_recv,
        c_send, c_recv, p_send, p_recv, t_send, t_recv, z_send, z_recv,
    ) = scratch[chunks + 10 :]

    grp = lax.axis_index("grp")
    seq = lax.axis_index("seq")
    core = lax.rem(seq, 2)
    chip = seq // 2
    sibling = seq + 1 - 2 * core

    def group_peer(step):
        return lax.rem(grp + step, groups)

    def chip_peer(step):
        return lax.rem(chip + step, chips)

    def cache_copy(b):
        return pltpu.make_async_copy(cache_ref.at[b], cache.at[b], cache_sem.at[b])

    for b in range(batch):
        cache_copy(b).start()

    peers = [(group_peer(k), seq) for k in range(1, groups)]
    peers += [(grp, chip_peer(k) * 2 + core) for k in range(1, chips)]
    peers += [(grp, sibling)]
    barrier = pltpu.get_barrier_semaphore()
    for peer in peers:
        pl.semaphore_signal(barrier, inc=1, device_id=peer, device_id_type=MESH)

    held = jnp.int32(0)
    for k in range(groups):
        held = jnp.where(owner_ref[k] == grp, k, held)
    for n in range(chunks):
        gathered[n][seq, grp] = query_ref[n, held]
    pl.semaphore_wait(barrier, len(peers))

    def remote(src, dst, send, recv, peer):
        return pltpu.make_async_remote_copy(
            src_ref=src, dst_ref=dst, send_sem=send, recv_sem=recv,
            device_id=peer, device_id_type=MESH,
        )

    def zq(n, k):
        ref = gathered[n].at[seq, grp]
        return remote(ref, ref, zq_send.at[n, k - 1], zq_recv.at[n, k - 1], (group_peer(k), seq))

    def pq(n, k):
        ref = gathered[n].at[seq]
        return remote(
            ref, ref, pq_send.at[n, k - 1], pq_recv.at[n, k - 1], (grp, chip_peer(k) * 2 + core)
        )

    def sq(n, k):
        ref = gathered[n].at[chip_peer(chips - k) * 2 + core]
        return remote(ref, ref, sq_send.at[n, k], sq_recv.at[n, k], (grp, sibling))

    def c_copy(b):
        return remote(
            packed.at[b, 1 - core], core_in.at[b], c_send.at[b], c_recv.at[b], (grp, sibling)
        )

    def p_copy(b, k):
        return remote(
            code_out.at[b, chip_peer(k)], code_in.at[b, k - 1],
            p_send.at[b, k - 1], p_recv.at[b, k - 1], (grp, chip_peer(k) * 2 + core),
        )

    def t_copy(b, k):
        return remote(
            plane_out.at[b, chip_peer(k), :, latent:], tail_in.at[b, k - 1],
            t_send.at[b, k - 1], t_recv.at[b, k - 1], (grp, chip_peer(k) * 2 + core),
        )

    def z_copy(b, k):
        return remote(
            group_out.at[b, group_peer(k)], group_in.at[b, k - 1],
            z_send.at[b, k - 1], z_recv.at[b, k - 1], (group_peer(k), seq),
        )

    def forward(n):
        for k in range(1, chips):
            pq(n, k).wait_recv()
            sq(n, k).start()

    for k in range(1, groups):
        zq(0, k).start()
    for n in range(chunks):
        for k in range(1, groups):
            zq(n, k).wait_recv()
        for k in range(1, chips):
            pq(n, k).start()
        sq(n, 0).start()
        if n + 1 < chunks:
            for k in range(1, groups):
                zq(n + 1, k).start()
        if n == 0:
            forward(0)

    blocks = groups * seqs
    rank = grp * seqs + seq
    stripe = slots // 2
    log_scale = softmax_scale * LOG2E

    def plane_stage(at):
        c_copy(at).wait_recv()
        top, total, output = merge([packed[at, core], core_in[at]], latent)
        plane_out[at, :, :, :latent] = output
        unit = jnp.max(jnp.abs(output), axis=-1, keepdims=True) * (1.0 / 32767.0)
        unit = jnp.maximum(unit, 1e-37)
        code_out[at] = jnp.round(output / unit).astype(jnp.int32).astype(jnp.int16)
        tail = pack_tail(top, total)
        lane = lax.broadcasted_iota(jnp.int32, tail.shape, 2)
        plane_out[at, :, :, latent:] = jnp.where(lane == TAIL - 1, unit, tail)
        for k in range(1, chips):
            t_copy(at, k).start()
            p_copy(at, k).start()

    def step(b, carry):
        @pl.when(b < batch)
        def _():
            for n in range(chunks):
                @pl.when(b == n * per_chunk)
                def _():
                    for k in range(chips):
                        sq(n, k).wait_recv()

                @pl.when(b // per_chunk == n)
                def _():
                    whole = []
                    for t in range(drafts):
                        row = b * drafts + t
                        owner = owner_ref[lax.rem(row, groups)]
                        whole.append(gathered[n][:, owner].reshape(rows // drafts, width))
                    stacked = jnp.concatenate(whole, axis=0)
                    query[...] = jnp.dot(
                        order_ref[...], stacked, preferred_element_type=jnp.float32
                    ).astype(jnp.bfloat16)

            cache_copy(b).wait()
            scores = jnp.dot(query[...], cache[b], preferred_element_type=jnp.float32)

            @pl.when(b >= 1)
            def _():
                plane_stage(b - 1)

            offset = lax.broadcasted_iota(jnp.int32, (1, slots), 1)
            position = jnp.where(
                offset < stripe,
                rank * stripe + offset,
                (2 * blocks - 1 - rank) * stripe + offset - stripe,
            )
            row_index = lax.broadcasted_iota(jnp.int32, (rows, 1), 0)
            draft = lax.rem(row_index, rows_per) // heads_per
            limit = lengths_ref[b] - drafts + 1 + draft
            scores = jnp.where(position < limit, scores, masked_score)
            top = jnp.maximum(jnp.max(scores, axis=1, keepdims=True), 0.1 * masked_score)
            weights = jnp.exp2((scores - top) * log_scale)
            total = jnp.sum(weights, axis=1, keepdims=True)
            output = lax.dot_general(
                weights.astype(jnp.bfloat16), cache[b, :latent], (((1,), (1,)), ((), ())),
                preferred_element_type=jnp.float32,
            )
            split = (2, chips, groups * rows_per)
            packed[b, :, :, :, :latent] = output.reshape(split + (latent,))
            packed[b, :, :, :, latent:] = pack_tail(top * log_scale, total).reshape(split + (TAIL,))
            c_copy(b).start()

            for n in range(1, chunks):
                @pl.when(b == n * per_chunk - 1)
                def _():
                    forward(n)

        @pl.when(b == batch)
        def _():
            plane_stage(b - 1)

        @pl.when((b >= 2) & (b < batch + 2))
        def _():
            at = b - 2
            for k in range(1, chips):
                t_copy(at, k).wait_recv()
                p_copy(at, k).wait_recv()
            parts = [plane_out[at, chip]]
            for k in range(chips - 1):
                tail = tail_in[at, k]
                values = code_in[at, k].astype(jnp.int32).astype(jnp.float32) * tail[:, TAIL - 1 :]
                parts.append(jnp.concatenate([values, tail], axis=1))
            top, total, output = merge(parts, latent)
            group_out[at, :, :, :latent] = output.reshape(groups, rows_per, latent)
            group_out[at, :, :, latent:] = pack_tail(top, total).reshape(groups, rows_per, TAIL)
            for k in range(1, groups):
                z_copy(at, k).start()

        @pl.when(b >= 3)
        def _():
            at = b - 3
            for k in range(1, groups):
                z_copy(at, k).wait_recv()
            parts = [group_out[at, grp]] + [group_in[at, k] for k in range(groups - 1)]
            top, total, output = merge(parts, latent)
            out_ref[at] = output / total
            c_copy(at).wait_send()
            for k in range(1, chips):
                t_copy(at, k).wait_send()
                p_copy(at, k).wait_send()
            for k in range(1, groups):
                z_copy(at, k).wait_send()

        return carry

    lax.fori_loop(0, batch + 3, step, 0)
    for n in range(chunks):
        for k in range(1, groups):
            zq(n, k).wait_send()
        for k in range(1, chips):
            pq(n, k).wait_send()
        for k in range(chips):
            sq(n, k).wait_send()


def row_order(drafts, groups, seqs, heads_per):
    heads = groups * seqs * heads_per
    source = np.arange(drafts * heads).reshape(drafts, groups, seqs // 2, 2, heads_per)
    source = source.transpose(3, 2, 1, 0, 4).reshape(-1)
    return (source[:, None] == np.arange(drafts * heads)[None, :]).astype(np.float32)


def fused_shards(queries, latent_cache, lengths, owner_group):
    seqs = lax.axis_size("seq")
    groups = lax.axis_size("grp")
    _, batch, drafts, part_heads, width = queries.shape
    slots = latent_cache.shape[1]
    latent = LATENT_WIDTH
    heads_per = part_heads // groups
    chunks = batch * drafts // groups
    chips = seqs // 2
    rows_per = drafts * heads_per
    rows = rows_per * groups * seqs
    dims = (batch, drafts, groups, seqs, chunks, heads_per, slots, width, latent)
    wide = latent + TAIL
    order = jnp.asarray(row_order(drafts, groups, seqs, heads_per), jnp.bfloat16)
    f32, bf16 = jnp.float32, jnp.bfloat16
    dma = pltpu.SemaphoreType.DMA
    out = pl.pallas_call(
        functools.partial(fused_kernel, dims),
        out_shape=jax.ShapeDtypeStruct((batch, rows_per, latent), f32),
        in_specs=[
            pl.BlockSpec(memory_space=pltpu.SMEM),
            pl.BlockSpec(memory_space=pltpu.SMEM),
            pl.BlockSpec(memory_space=pltpu.VMEM),
            pl.BlockSpec(memory_space=pltpu.VMEM),
            pl.BlockSpec(memory_space=pl.ANY),
        ],
        out_specs=pl.BlockSpec(memory_space=pltpu.VMEM),
        scratch_shapes=[pltpu.VMEM((seqs, groups, part_heads, width), bf16)] * chunks
        + [
            pltpu.VMEM((batch, width, slots), bf16),
            pltpu.VMEM((rows, width), bf16),
            pltpu.VMEM((batch, 2, chips, groups * rows_per, wide), f32),
            pltpu.VMEM((batch, chips, groups * rows_per, wide), f32),
            pltpu.VMEM((batch, chips, groups * rows_per, wide), f32),
            pltpu.VMEM((batch, chips - 1, groups * rows_per, TAIL), f32),
            pltpu.VMEM((batch, chips, groups * rows_per, latent), jnp.int16),
            pltpu.VMEM((batch, chips - 1, groups * rows_per, latent), jnp.int16),
            pltpu.VMEM((batch, groups, rows_per, wide), f32),
            pltpu.VMEM((batch, groups - 1, rows_per, wide), f32),
            dma((batch,)),
            dma((chunks, groups - 1)), dma((chunks, groups - 1)),
            dma((chunks, chips - 1)), dma((chunks, chips - 1)),
            dma((chunks, chips)), dma((chunks, chips)),
            dma((batch,)), dma((batch,)),
            dma((batch, chips - 1)), dma((batch, chips - 1)),
            dma((batch, chips - 1)), dma((batch, chips - 1)),
            dma((batch, groups - 1)), dma((batch, groups - 1)),
        ],
        compiler_params=pltpu.CompilerParams(
            collective_id=0, has_side_effects=True, vmem_limit_bytes=48 * 1024 * 1024
        ),
    )(lengths, owner_group, queries.reshape(chunks, groups, part_heads, width), order, latent_cache.transpose(0, 2, 1))
    return out.reshape(batch, drafts, heads_per, latent).astype(bf16)


def fits_kernel(mesh):
    seqs, groups = mesh.shape["seq"], mesh.shape["grp"]

    def check(queries):
        _, batch, drafts, heads, _ = queries.shape
        parts = seqs * groups
        rows = batch * drafts
        return (
            seqs % 2 == 0 and seqs > 2 and groups > 1
            and heads % parts == 0 and (heads // parts * drafts) % 8 == 0
            and (heads // seqs) % 16 == 0
            and rows % groups == 0 and batch % (rows // groups) == 0
        )

    return check


def block_partial(query_matrix, cache_block, limits, block_rank, blocks):
    batch, rows, width = query_matrix.shape
    slots = cache_block.shape[1]
    stripe = slots // 2
    drafts = limits.shape[1]
    heads = rows // drafts
    offset = jnp.arange(slots, dtype=jnp.int32)
    position = jnp.where(
        offset < stripe,
        block_rank * stripe + offset,
        (2 * blocks - 1 - block_rank) * stripe + offset - stripe,
    )
    valid_slot = position[None, None, :] < limits[:, :, None]
    logit_scores = (
        jnp.einsum("fdi,fei->fde", query_matrix, cache_block, preferred_element_type=jnp.float32)
        * softmax_scale
    )
    logit_scores = logit_scores.reshape(batch, drafts, heads, slots)
    logit_scores = jnp.where(valid_slot[:, :, None, :], logit_scores, masked_score)
    local_max = jnp.max(logit_scores, axis=3)
    weights = jnp.where(
        valid_slot[:, :, None, :], jnp.exp(logit_scores - local_max[..., None]), 0.0
    )
    local_sum = jnp.sum(weights, axis=3)
    rounded_values = weights.astype(jnp.bfloat16).reshape(batch, rows, slots)
    partial_output = jnp.einsum(
        "giv,gvu->giu",
        rounded_values,
        cache_block[:, :, :LATENT_WIDTH],
        preferred_element_type=jnp.float32,
    )
    return (local_max, local_sum, partial_output.reshape(batch, drafts, heads, LATENT_WIDTH))


def owned_rows(copies, owner_group, group_count, group_rank):
    batch, drafts = (copies.shape[1], copies.shape[2])
    row_index = jnp.arange(batch * drafts, dtype=jnp.int32) % group_count
    owners = jnp.take(owner_group, row_index).reshape(batch, drafts)
    mine = owners == group_rank
    return jnp.where(mine[None, :, :, None, None], copies.astype(jnp.float32), 0.0)


def shards(queries, latent_cache, lengths, owner_group):
    seq_count = lax.axis_size("seq")
    group_count = lax.axis_size("grp")
    blocks = seq_count * group_count
    group_rank = lax.axis_index("grp")
    device_rank = group_rank * seq_count + lax.axis_index("seq")
    kept = owned_rows(queries, owner_group, group_count, group_rank)
    own_heads = lax.psum(kept.astype(jnp.bfloat16), "grp")
    gathered = lax.all_gather(own_heads, "seq", axis=3, tiled=True)
    batch, drafts, heads, width = gathered.shape[1:]
    query_matrix = gathered.reshape(batch, drafts * heads, width)
    limits = lengths[:, None] - drafts + 1 + jnp.arange(drafts, dtype=jnp.int32)[None, :]
    local_parts = block_partial(query_matrix, latent_cache, limits, device_rank, blocks)
    local_max, local_sum, partial_output = local_parts
    highest = lax.pmax(local_max, ("grp", "seq"))
    factor = jnp.exp(local_max - highest)
    total, summed = (
        lax.psum_scatter(local_sum * factor, ("grp", "seq"), scatter_dimension=2, tiled=True),
        lax.psum_scatter(
            partial_output * factor[..., None], ("grp", "seq"), scatter_dimension=2, tiled=True
        ),
    )
    return (summed / total[..., None]).astype(jnp.bfloat16)


def solution(mesh):
    check = fits_kernel(mesh)

    def attend(queries, latent_cache, lengths, owner_group):
        return jax.shard_map(
            fused_shards if check(queries) else shards,
            mesh=mesh,
            in_specs=(P("grp", None, None, "seq", None), P(None, ("grp", "seq"), None), P(), P()),
            out_specs=P(None, None, ("grp", "seq"), None),
            check_vma=False,
        )(queries, latent_cache, lengths, owner_group)

    return attend
```

```python
import functools

import jax
import jax.numpy as jnp
import numpy as np
from jax import lax
from jax.experimental import pallas as pl
from jax.experimental.pallas import tpu as pltpu
from jax.sharding import PartitionSpec as P

LATENT_WIDTH = 512
LOG2E = 1.4426950408889634
MESH = pl.DeviceIdType.MESH
TAIL = 128


softmax_scale = 192.0 ** (-0.5)
masked_score = -1e30


def merge(parts, latent):
    tops = [part[..., latent + TAIL // 2 : latent + TAIL // 2 + 1] for part in parts]
    top = functools.reduce(jnp.maximum, tops)
    total, output = None, None
    for part, own_top in zip(parts, tops):
        factor = jnp.exp2(own_top - top)
        part_sum = part[..., latent : latent + 1] * factor
        part_output = part[..., :latent] * factor
        total = part_sum if total is None else total + part_sum
        output = part_output if output is None else output + part_output
    return top, total, output


def pack_tail(top, total):
    shape = top.shape[:-1] + (TAIL,)
    lane = lax.broadcasted_iota(jnp.int32, shape, len(shape) - 1)
    return jnp.where(
        lane < TAIL // 2, jnp.broadcast_to(total, shape), jnp.broadcast_to(top, shape)
    )


def fused_kernel(dims, lengths_ref, owner_ref, query_ref, order_ref, cache_ref, out_ref, *scratch):
    batch, drafts, groups, seqs, chunks, heads_per, slots, width, latent = dims
    chips = seqs // 2
    per_chunk = batch // chunks
    rows_per = drafts * heads_per
    rows = drafts * heads_per * groups * seqs
    gathered = scratch[:chunks]
    (
        cache, query, packed, core_in, plane_out, tail_in, code_out, code_in, group_out, group_in,
    ) = scratch[chunks : chunks + 10]
    (
        cache_sem,
        zq_send, zq_recv, pq_send, pq_recv, sq_send, sq_recv,
        c_send, c_recv, p_send, p_recv, t_send, t_recv, z_send, z_recv,
    ) = scratch[chunks + 10 :]

    grp = lax.axis_index("grp")
    seq = lax.axis_index("seq")
    core = lax.rem(seq, 2)
    chip = seq // 2
    sibling = seq + 1 - 2 * core

    def group_peer(step):
        return lax.rem(grp + step, groups)

    def chip_peer(step):
        return lax.rem(chip + step, chips)

    def cache_copy(b):
        return pltpu.make_async_copy(cache_ref.at[b], cache.at[b], cache_sem.at[b])

    peers = [(group_peer(k), seq) for k in range(1, groups)]
    peers += [(grp, chip_peer(k) * 2 + core) for k in range(1, chips)]
    peers += [(grp, sibling)]
    barrier = pltpu.get_barrier_semaphore()
    for peer in peers:
        pl.semaphore_signal(barrier, inc=1, device_id=peer, device_id_type=MESH)

    for b in range(batch):
        cache_copy(b).start()

    held = jnp.int32(0)
    for k in range(groups):
        held = jnp.where(owner_ref[k] == grp, k, held)
    for n in range(chunks):
        gathered[n][seq, grp] = query_ref[n, held]
    pl.semaphore_wait(barrier, len(peers))

    def remote(src, dst, send, recv, peer):
        return pltpu.make_async_remote_copy(
            src_ref=src, dst_ref=dst, send_sem=send, recv_sem=recv,
            device_id=peer, device_id_type=MESH,
        )

    def zq(n, k):
        ref = gathered[n].at[seq, grp]
        return remote(ref, ref, zq_send.at[n, k - 1], zq_recv.at[n, k - 1], (group_peer(k), seq))

    def pq(n, k, j):
        ref = gathered[n].at[seq, group_peer(groups - j)]
        return remote(
            ref, ref, pq_send.at[n, k - 1, j], pq_recv.at[n, k - 1, j],
            (grp, chip_peer(k) * 2 + core),
        )

    def sq(n, k):
        ref = gathered[n].at[chip_peer(chips - k) * 2 + core]
        return remote(ref, ref, sq_send.at[n, k], sq_recv.at[n, k], (grp, sibling))

    def c_copy(b):
        return remote(
            packed.at[b, 1 - core], core_in.at[b], c_send.at[b], c_recv.at[b], (grp, sibling)
        )

    def p_copy(b, k):
        return remote(
            code_out.at[b, chip_peer(k)], code_in.at[b, k - 1],
            p_send.at[b, k - 1], p_recv.at[b, k - 1], (grp, chip_peer(k) * 2 + core),
        )

    def t_copy(b, k):
        return remote(
            plane_out.at[b, chip_peer(k), :, latent:], tail_in.at[b, k - 1],
            t_send.at[b, k - 1], t_recv.at[b, k - 1], (grp, chip_peer(k) * 2 + core),
        )

    def z_copy(b, k):
        return remote(
            group_out.at[b, group_peer(k)], group_in.at[b, k - 1],
            z_send.at[b, k - 1], z_recv.at[b, k - 1], (group_peer(k), seq),
        )

    def forward(n):
        for k in range(1, chips):
            for j in range(groups):
                pq(n, k, j).wait_recv()
            sq(n, k).start()

    for k in range(1, groups):
        zq(0, k).start()
    for n in range(chunks):
        for j in range(groups):
            if j:
                zq(n, j).wait_recv()
            for k in range(1, chips):
                pq(n, k, j).start()
        sq(n, 0).start()
        if n + 1 < chunks:
            for k in range(1, groups):
                zq(n + 1, k).start()
        if n == 0:
            forward(0)

    blocks = groups * seqs
    rank = grp * seqs + seq
    stripe = slots // 2
    log_scale = softmax_scale * LOG2E

    def plane_stage(at):
        c_copy(at).wait_recv()
        top, total, output = merge([packed[at, core], core_in[at]], latent)
        plane_out[at, :, :, :latent] = output
        unit = jnp.max(jnp.abs(output), axis=-1, keepdims=True) * (1.0 / 32767.0)
        unit = jnp.maximum(unit, 1e-37)
        code_out[at] = jnp.round(output / unit).astype(jnp.int32).astype(jnp.int16)
        tail = pack_tail(top, total)
        lane = lax.broadcasted_iota(jnp.int32, tail.shape, 2)
        plane_out[at, :, :, latent:] = jnp.where(lane == TAIL - 1, unit, tail)
        for k in range(1, chips):
            t_copy(at, k).start()
            p_copy(at, k).start()

    def step(b, carry):
        @pl.when(b < batch)
        def _():
            for n in range(chunks):
                @pl.when(b == n * per_chunk)
                def _():
                    for k in range(chips):
                        sq(n, k).wait_recv()

                @pl.when(b // per_chunk == n)
                def _():
                    whole = []
                    for t in range(drafts):
                        row = b * drafts + t
                        owner = owner_ref[lax.rem(row, groups)]
                        whole.append(gathered[n][:, owner].reshape(rows // drafts, width))
                    stacked = jnp.concatenate(whole, axis=0)
                    query[...] = jnp.dot(
                        order_ref[...], stacked, preferred_element_type=jnp.float32
                    ).astype(jnp.bfloat16)

            cache_copy(b).wait()
            scores = jnp.dot(query[...], cache[b], preferred_element_type=jnp.float32)

            @pl.when(b >= 1)
            def _():
                plane_stage(b - 1)

            offset = lax.broadcasted_iota(jnp.int32, (1, slots), 1)
            position = jnp.where(
                offset < stripe,
                rank * stripe + offset,
                (2 * blocks - 1 - rank) * stripe + offset - stripe,
            )
            row_index = lax.broadcasted_iota(jnp.int32, (rows, 1), 0)
            draft = lax.rem(row_index, rows_per) // heads_per
            limit = lengths_ref[b] - drafts + 1 + draft
            scores = jnp.where(position < limit, scores, masked_score)
            top = jnp.maximum(jnp.max(scores, axis=1, keepdims=True), 0.1 * masked_score)
            weights = jnp.exp2((scores - top) * log_scale)
            total = jnp.sum(weights, axis=1, keepdims=True)
            output = lax.dot_general(
                weights.astype(jnp.bfloat16), cache[b, :latent], (((1,), (1,)), ((), ())),
                preferred_element_type=jnp.float32,
            )
            split = (2, chips, groups * rows_per)
            packed[b, :, :, :, :latent] = output.reshape(split + (latent,))
            packed[b, :, :, :, latent:] = pack_tail(top * log_scale, total).reshape(split + (TAIL,))
            c_copy(b).start()

            for n in range(1, chunks):
                @pl.when(b == n * per_chunk - 1)
                def _():
                    forward(n)

        @pl.when(b == batch)
        def _():
            plane_stage(b - 1)

        @pl.when((b >= 2) & (b < batch + 2))
        def _():
            at = b - 2
            for k in range(1, chips):
                t_copy(at, k).wait_recv()
                p_copy(at, k).wait_recv()
            parts = [plane_out[at, chip]]
            for k in range(chips - 1):
                tail = tail_in[at, k]
                values = code_in[at, k].astype(jnp.int32).astype(jnp.float32) * tail[:, TAIL - 1 :]
                parts.append(jnp.concatenate([values, tail], axis=1))
            top, total, output = merge(parts, latent)
            group_out[at, :, :, :latent] = output.reshape(groups, rows_per, latent)
            group_out[at, :, :, latent:] = pack_tail(top, total).reshape(groups, rows_per, TAIL)
            for k in range(1, groups):
                z_copy(at, k).start()

        @pl.when(b >= 3)
        def _():
            at = b - 3
            for k in range(1, groups):
                z_copy(at, k).wait_recv()
            parts = [group_out[at, grp]] + [group_in[at, k] for k in range(groups - 1)]
            top, total, output = merge(parts, latent)
            out_ref[at] = output / total
            c_copy(at).wait_send()
            for k in range(1, chips):
                t_copy(at, k).wait_send()
                p_copy(at, k).wait_send()
            for k in range(1, groups):
                z_copy(at, k).wait_send()

        return carry

    lax.fori_loop(0, batch + 3, step, 0)
    for n in range(chunks):
        for k in range(1, groups):
            zq(n, k).wait_send()
        for k in range(1, chips):
            for j in range(groups):
                pq(n, k, j).wait_send()
        for k in range(chips):
            sq(n, k).wait_send()


def row_order(drafts, groups, seqs, heads_per):
    heads = groups * seqs * heads_per
    source = np.arange(drafts * heads).reshape(drafts, groups, seqs // 2, 2, heads_per)
    source = source.transpose(3, 2, 1, 0, 4).reshape(-1)
    return (source[:, None] == np.arange(drafts * heads)[None, :]).astype(np.float32)


def fused_shards(queries, latent_cache, lengths, owner_group):
    seqs = lax.axis_size("seq")
    groups = lax.axis_size("grp")
    _, batch, drafts, part_heads, width = queries.shape
    slots = latent_cache.shape[1]
    latent = LATENT_WIDTH
    heads_per = part_heads // groups
    chunks = batch * drafts // groups
    chips = seqs // 2
    rows_per = drafts * heads_per
    rows = rows_per * groups * seqs
    dims = (batch, drafts, groups, seqs, chunks, heads_per, slots, width, latent)
    wide = latent + TAIL
    order = jnp.asarray(row_order(drafts, groups, seqs, heads_per), jnp.bfloat16)
    f32, bf16 = jnp.float32, jnp.bfloat16
    dma = pltpu.SemaphoreType.DMA
    out = pl.pallas_call(
        functools.partial(fused_kernel, dims),
        out_shape=jax.ShapeDtypeStruct((batch, rows_per, latent), f32),
        in_specs=[
            pl.BlockSpec(memory_space=pltpu.SMEM),
            pl.BlockSpec(memory_space=pltpu.SMEM),
            pl.BlockSpec(memory_space=pltpu.VMEM),
            pl.BlockSpec(memory_space=pltpu.VMEM),
            pl.BlockSpec(memory_space=pl.ANY),
        ],
        out_specs=pl.BlockSpec(memory_space=pltpu.VMEM),
        scratch_shapes=[pltpu.VMEM((seqs, groups, part_heads, width), bf16)] * chunks
        + [
            pltpu.VMEM((batch, width, slots), bf16),
            pltpu.VMEM((rows, width), bf16),
            pltpu.VMEM((batch, 2, chips, groups * rows_per, wide), f32),
            pltpu.VMEM((batch, chips, groups * rows_per, wide), f32),
            pltpu.VMEM((batch, chips, groups * rows_per, wide), f32),
            pltpu.VMEM((batch, chips - 1, groups * rows_per, TAIL), f32),
            pltpu.VMEM((batch, chips, groups * rows_per, latent), jnp.int16),
            pltpu.VMEM((batch, chips - 1, groups * rows_per, latent), jnp.int16),
            pltpu.VMEM((batch, groups, rows_per, wide), f32),
            pltpu.VMEM((batch, groups - 1, rows_per, wide), f32),
            dma((batch,)),
            dma((chunks, groups - 1)), dma((chunks, groups - 1)),
            dma((chunks, chips - 1, groups)), dma((chunks, chips - 1, groups)),
            dma((chunks, chips)), dma((chunks, chips)),
            dma((batch,)), dma((batch,)),
            dma((batch, chips - 1)), dma((batch, chips - 1)),
            dma((batch, chips - 1)), dma((batch, chips - 1)),
            dma((batch, groups - 1)), dma((batch, groups - 1)),
        ],
        compiler_params=pltpu.CompilerParams(
            collective_id=0, has_side_effects=True, vmem_limit_bytes=48 * 1024 * 1024
        ),
    )(lengths, owner_group, queries.reshape(chunks, groups, part_heads, width), order, latent_cache.transpose(0, 2, 1))
    return out.reshape(batch, drafts, heads_per, latent).astype(bf16)


def fits_kernel(mesh):
    seqs, groups = mesh.shape["seq"], mesh.shape["grp"]

    def check(queries):
        _, batch, drafts, heads, _ = queries.shape
        parts = seqs * groups
        rows = batch * drafts
        return (
            seqs % 2 == 0 and seqs > 2 and groups > 1
            and heads % parts == 0 and (heads // parts * drafts) % 8 == 0
            and (heads // seqs) % 16 == 0
            and rows % groups == 0 and batch % (rows // groups) == 0
        )

    return check


def block_partial(query_matrix, cache_block, limits, block_rank, blocks):
    batch, rows, width = query_matrix.shape
    slots = cache_block.shape[1]
    stripe = slots // 2
    drafts = limits.shape[1]
    heads = rows // drafts
    offset = jnp.arange(slots, dtype=jnp.int32)
    position = jnp.where(
        offset < stripe,
        block_rank * stripe + offset,
        (2 * blocks - 1 - block_rank) * stripe + offset - stripe,
    )
    valid_slot = position[None, None, :] < limits[:, :, None]
    logit_scores = (
        jnp.einsum("fdi,fei->fde", query_matrix, cache_block, preferred_element_type=jnp.float32)
        * softmax_scale
    )
    logit_scores = logit_scores.reshape(batch, drafts, heads, slots)
    logit_scores = jnp.where(valid_slot[:, :, None, :], logit_scores, masked_score)
    local_max = jnp.max(logit_scores, axis=3)
    weights = jnp.where(
        valid_slot[:, :, None, :], jnp.exp(logit_scores - local_max[..., None]), 0.0
    )
    local_sum = jnp.sum(weights, axis=3)
    rounded_values = weights.astype(jnp.bfloat16).reshape(batch, rows, slots)
    partial_output = jnp.einsum(
        "giv,gvu->giu",
        rounded_values,
        cache_block[:, :, :LATENT_WIDTH],
        preferred_element_type=jnp.float32,
    )
    return (local_max, local_sum, partial_output.reshape(batch, drafts, heads, LATENT_WIDTH))


def owned_rows(copies, owner_group, group_count, group_rank):
    batch, drafts = (copies.shape[1], copies.shape[2])
    row_index = jnp.arange(batch * drafts, dtype=jnp.int32) % group_count
    owners = jnp.take(owner_group, row_index).reshape(batch, drafts)
    mine = owners == group_rank
    return jnp.where(mine[None, :, :, None, None], copies.astype(jnp.float32), 0.0)


def shards(queries, latent_cache, lengths, owner_group):
    seq_count = lax.axis_size("seq")
    group_count = lax.axis_size("grp")
    blocks = seq_count * group_count
    group_rank = lax.axis_index("grp")
    device_rank = group_rank * seq_count + lax.axis_index("seq")
    kept = owned_rows(queries, owner_group, group_count, group_rank)
    own_heads = lax.psum(kept.astype(jnp.bfloat16), "grp")
    gathered = lax.all_gather(own_heads, "seq", axis=3, tiled=True)
    batch, drafts, heads, width = gathered.shape[1:]
    query_matrix = gathered.reshape(batch, drafts * heads, width)
    limits = lengths[:, None] - drafts + 1 + jnp.arange(drafts, dtype=jnp.int32)[None, :]
    local_parts = block_partial(query_matrix, latent_cache, limits, device_rank, blocks)
    local_max, local_sum, partial_output = local_parts
    highest = lax.pmax(local_max, ("grp", "seq"))
    factor = jnp.exp(local_max - highest)
    total, summed = (
        lax.psum_scatter(local_sum * factor, ("grp", "seq"), scatter_dimension=2, tiled=True),
        lax.psum_scatter(
            partial_output * factor[..., None], ("grp", "seq"), scatter_dimension=2, tiled=True
        ),
    )
    return (summed / total[..., None]).astype(jnp.bfloat16)


def solution(mesh):
    check = fits_kernel(mesh)

    def attend(queries, latent_cache, lengths, owner_group):
        return jax.shard_map(
            fused_shards if check(queries) else shards,
            mesh=mesh,
            in_specs=(P("grp", None, None, "seq", None), P(None, ("grp", "seq"), None), P(), P()),
            out_specs=P(None, None, ("grp", "seq"), None),
            check_vma=False,
        )(queries, latent_cache, lengths, owner_group)

    return attend
```
